32 devices in a mesh: dp: 4 (over y, x), row: 4 (over z), col: 2 (over core).
Axes of the slice: x: 2, y: 2, z: 4, core: 2. Of those that a mesh axis runs over, the one named last changes fastest.
Arguments:
- tokens: bfloat16 [8, 2048, 1024], P(('dp', 'col'), 'row'), may hold values from -6 to 6
- segments: int32 [8, 2048], P(('dp', 'col'), 'row'), may hold values from 0 to 2, as said below
- gain_attn: float32 [1024], replicated, may hold values from 0.1 to 1.9
- w_qkv: bfloat16 [3, 1024, 1024], P(None, 'col', 'row'), may hold values from -0.1875 to 0.1875
- w_attn_out: bfloat16 [1024, 1024], P('col', 'row'), may hold values from -0.75 to 0.75
- gain_mlp: float32 [1024], replicated, may hold values from 0.1 to 1.9
- w_in: bfloat16 [2, 2624, 1024], P(None, 'col', 'row'), may hold values from -0.1875 to 0.1875
- w_mlp: bfloat16 [2624, 1024], P('col', 'row'), may hold values from -0.125 to 0.125
- cotangent: bfloat16 [8, 2048, 1024], P(('dp', 'col'), 'row'), may hold values from -6 to 6
Outputs:
- output: bfloat16 [8, 2048, 1024], P(('dp', 'col'), 'row')
- grad_input: bfloat16 [8, 2048, 1024], P(('dp', 'col'), 'row')
- grad_w_qkv: float32 [3, 1024, 1024], P(None, 'col', 'row')
- grad_w_attn_out: float32 [1024, 1024], P('col', 'row')
- grad_w_in: float32 [2, 2624, 1024], P(None, 'col', 'row')
- grad_w_mlp: float32 [2624, 1024], P('col', 'row')
- grad_gain_attn: float32 [1024], P(('row', 'col'))
- grad_gain_mlp: float32 [1024], P(('row', 'col'))
The draws below stay inside these ranges and needn't reach their ends.
Inputs may be any that keep to these rules, and one draw needn't show every extreme that they name: `segments`: along each sequence the ids never fall; a token attends only to tokens of its sequence with the same id.
All inputs are finite; a program needn't handle non-finite values.
Results may differ from the reference program's by a relative error of at most 0.015.
Values may be sent and summed in bfloat16 or wider, within the bound.
A program may use at most 384 MiB of HBM per device.

```python
import jax
import jax.numpy as jnp
from jax import lax

D = 1024
HEADS = 16
HEAD = 64
FF = 2624
SEQ_LEN = 2048
BATCH = 8


def draw_segments(key, part):
    key = jax.random.fold_in(key, 7)
    start_key, end_key = jax.random.split(key)
    starts = jax.random.randint(start_key, (BATCH, 1), SEQ_LEN // 10, SEQ_LEN // 8 + 1)
    ends = jax.random.randint(end_key, (BATCH, 1), SEQ_LEN - SEQ_LEN // 8, SEQ_LEN - SEQ_LEN // 10 + 1)
    positions = jnp.arange(SEQ_LEN, dtype=jnp.int32)[None, :]
    return (positions >= starts).astype(jnp.int32) + (positions >= ends).astype(jnp.int32)


def levels(key, extent, cuts, low, largest):
    level, own = 1.0, jax.random.fold_in(key, 6)
    for dim, parts in cuts:
        draws = jnp.exp(jax.random.uniform(jax.random.fold_in(own, dim), (parts,), jnp.float32, low / len(cuts), largest / len(cuts)))
        level = level * jnp.repeat(draws, extent[dim] // parts).reshape([-1 if axis == dim else 1 for axis in range(len(extent))])
    return level


def normal_values(key, dims, width, limit, shards=(), kind=jnp.bfloat16):
    result = width * jax.random.normal(key, dims, jnp.float32)
    if shards:
        result = result * levels(key, dims, shards, -0.22, 0.18)
    return jnp.clip(result, -limit, limit).astype(kind)


def setup_inputs(seed: int = 0) -> dict:
    key_list = jax.random.split(jax.random.key(seed), 10)
    return {
        "tokens": normal_values(key_list[0], (BATCH, SEQ_LEN, D), 1.0, 6.0, ((0, 8), (1, 4))),
        "segments": draw_segments(jax.random.fold_in(key_list[9], 71), 0),
        "gain_attn": jnp.clip(1.0 + 0.18 * jax.random.normal(key_list[2], (D,), jnp.float32), 0.1, 1.9),
        "w_qkv": normal_values(key_list[3], (3, D, D), D ** -0.5, 0.1875, ((1, 2), (2, 4))),
        "w_attn_out": normal_values(key_list[4], (D, D), (D // 16) ** -0.5, 0.75, ((0, 2), (1, 4))),
        "gain_mlp": jnp.clip(1.0 + 0.18 * jax.random.normal(key_list[5], (D,), jnp.float32), 0.1, 1.9),
        "w_in": normal_values(key_list[6], (2, FF, D), D ** -0.5, 0.1875, ((1, 2), (2, 4))),
        "w_mlp": normal_values(key_list[7], (FF, D), FF ** -0.5, 0.125, ((0, 2), (1, 4))),
        "cotangent": normal_values(key_list[8], (BATCH, SEQ_LEN, D), 1.0, 6.0, ((0, 8), (1, 4))),
    }


@jax.custom_vjp
def low(v):
    return lax.optimization_barrier(v.astype(jnp.bfloat16)).astype(jnp.float32)

@jax.custom_vjp
def low_back(v):
    return v

def low_keep(v):
    return (low(v), None)

def low_pass(kept, grad):
    return (grad,)

def back_keep(v):
    return (v, None)

def back_low(kept, grad):
    return (low(grad),)
low.defvjp(low_keep, low_pass)
low_back.defvjp(back_keep, back_low)
EPSILON = 1e-05
ROPE_BASE = 160000.0
HIGHEST = lax.Precision.HIGHEST

def layer_norm(inputs, gain):
    average = lax.optimization_barrier(jnp.mean(inputs, axis=-1, keepdims=True))
    centred = inputs - average
    variance = lax.optimization_barrier(jnp.mean(centred * centred, axis=-1, keepdims=True))
    return centred * lax.rsqrt(variance + EPSILON) * gain

def rotary(positions):
    half_head = HEAD // 2
    frequency = jnp.power(ROPE_BASE, -2.0 * jnp.arange(half_head).astype(jnp.float32) / HEAD)
    angles = positions[:, None] * frequency[None, :]
    angles = jnp.concatenate([angles, angles], axis=-1)
    return (jnp.cos(angles), jnp.sin(angles))

def rope(inputs, cosine, sine_table):
    half_head = HEAD // 2
    turned = jnp.concatenate([-inputs[..., half_head:], inputs[..., :half_head]], axis=-1)
    return inputs * cosine[:, None, :] + turned * sine_table[:, None, :]

def attend_block(query_block, seg_block, key_heads, value_heads, seg_keys):
    raw_scores = jnp.einsum('qhe,khe->hqk', query_block, key_heads, precision=HIGHEST)
    logits = low_back(raw_scores) * HEAD ** (-0.5)
    allowed = seg_block[None, :, None] == seg_keys[None, None, :]
    logits = jnp.where(allowed, logits, -1e+30)
    highest = lax.optimization_barrier(jnp.max(logits, axis=-1, keepdims=True))
    exponent = jnp.exp(logits - highest)
    weights = exponent / lax.optimization_barrier(jnp.sum(exponent, axis=-1, keepdims=True))
    return jnp.einsum('hqk,khe->qhe', low(weights), value_heads, precision=HIGHEST)

def layer(inputs, gain_attn, w_qkv, w_attn_out, gain_mlp, w_in, w_mlp, seg_ids):
    norm_one = low(layer_norm(inputs, gain_attn))
    projected = low_back(jnp.dot(norm_one, w_qkv.reshape(3 * D, D).T, precision=HIGHEST))
    projected = projected.reshape(SEQ_LEN, 3, HEADS, HEAD)
    cosine, sine_table = rotary(jnp.arange(SEQ_LEN).astype(jnp.float32))
    query_heads = low(rope(projected[:, 0], cosine, sine_table))
    key_heads = low(rope(projected[:, 1], cosine, sine_table))
    value_heads = low(projected[:, 2])
    block_rows = min(512, SEQ_LEN)
    query_blocks = query_heads.reshape(SEQ_LEN // block_rows, block_rows, HEADS, HEAD)
    seg_blocks = seg_ids.reshape(SEQ_LEN // block_rows, block_rows)

    def run_block(element):
        return attend_block(element[0], element[1], key_heads, value_heads, seg_ids)
    attended = lax.map(jax.checkpoint(run_block), (query_blocks, seg_blocks))
    mixed = low_back(low(attended.reshape(SEQ_LEN, D)))
    residual = inputs + low_back(jnp.dot(mixed, w_attn_out.T, precision=HIGHEST))
    norm_two = low(layer_norm(residual, gain_mlp))
    lifted = low_back(jnp.dot(norm_two, w_in.reshape(2 * FF, D).T, precision=HIGHEST)).reshape(SEQ_LEN, 2, FF)
    gated = low(jax.nn.gelu(lifted[:, 0], approximate=False) * lifted[:, 1])
    return residual + low_back(jnp.dot(gated, w_mlp, precision=HIGHEST))

def reference(tokens, segments, gain_attn, w_qkv, w_attn_out, gain_mlp, w_in, w_mlp, cotangent):
    params = (gain_attn.astype(jnp.float32), w_qkv.astype(jnp.float32), w_attn_out.astype(jnp.float32), gain_mlp.astype(jnp.float32), w_in.astype(jnp.float32), w_mlp.astype(jnp.float32))

    def step(carry, element):
        seq_tokens, seq_ids, seq_cot = element

        def apply_layer(inputs, gain_one, qkv_weight, out_weight, gain_two, inner_weight, mlp_weight):
            return layer(inputs, gain_one, qkv_weight, out_weight, gain_two, inner_weight, mlp_weight, seq_ids)
        output_seq, pullback = jax.vjp(apply_layer, seq_tokens.astype(jnp.float32), *params)
        gradients = pullback(seq_cot.astype(jnp.float32))
        updated = tuple((before + after for before, after in zip(carry, gradients[1:])))
        return (updated, (output_seq.astype(jnp.bfloat16), gradients[0].astype(jnp.bfloat16)))
    initial = tuple((jnp.zeros_like(weight) for weight in params))
    totals, (output, grad_input) = lax.scan(step, initial, (tokens, segments, cotangent))
    return (output, grad_input, totals[1], totals[2], totals[4], totals[5], totals[0], totals[3])
```

```python
import jax
import jax.numpy as jnp
from jax import lax
from jax.experimental import pallas as pl
from jax.experimental.pallas import tpu as pltpu
from jax.sharding import PartitionSpec as P

HEADS = 16
HEAD = 64
EPSILON = 1e-05
ROPE_BASE = 160000.0
MASKED = -1e30
LOG2E = 1.4426950408889634
SCALE2 = HEAD ** (-0.5) * LOG2E
F32 = jnp.float32
BF16 = jnp.bfloat16
FQ, FK = 256, 512
BK, BQ = 256, 512


def layer_norm(inputs, gain):
    average = jnp.mean(inputs, axis=-1, keepdims=True)
    centred = inputs - average
    variance = jnp.mean(centred * centred, axis=-1, keepdims=True)
    return centred * lax.rsqrt(variance + EPSILON) * gain


def rotary(positions, heads):
    half_head = HEAD // 2
    frequency = jnp.power(ROPE_BASE, -2.0 * jnp.arange(half_head).astype(F32) / HEAD)
    angles = positions[:, None] * frequency[None, :]
    return (jnp.tile(jnp.cos(angles), (1, 2 * heads)), jnp.tile(jnp.sin(angles), (1, 2 * heads)))


def turned(flat):
    half = HEAD // 2
    ahead = jnp.concatenate([flat[:, half:], flat[:, :half]], axis=1)
    behind = jnp.concatenate([flat[:, -half:], flat[:, :-half]], axis=1)
    first = (lax.broadcasted_iota(jnp.int32, flat.shape, 1) % HEAD) < half
    return jnp.where(first, -ahead, behind)


def contract_rows(left_side, right_side):
    return lax.dot_general(
        left_side, right_side, (((0,), (0,)), ((), ())), preferred_element_type=F32
    )


def times_transpose(left_side, right_side):
    return lax.dot_general(
        left_side, right_side, (((1,), (1,)), ((), ())), preferred_element_type=F32
    )


def plain(left_side, right_side):
    return jnp.dot(left_side, right_side, preferred_element_type=F32)


def forward_kernel(bounds, q_ref, k_ref, vt_ref, segq_ref, segk_ref, o_ref, lse_ref, acc):
    block = pl.program_id(0)
    heads = lse_ref.shape[0]
    acc[...] = jnp.zeros_like(acc)
    seg_query = segq_ref[...]

    def step(tile, carry):
        rows = pl.ds(pl.multiple_of(tile * FK, FK), FK)
        allowed = segk_ref[rows, :] == seg_query
        kept = []
        for head in range(heads):
            highest, summed = carry[head]
            cols = slice(head * HEAD, (head + 1) * HEAD)
            logits = times_transpose(k_ref[rows, cols], q_ref[:, cols]) * SCALE2
            logits = jnp.where(allowed, logits, MASKED)
            higher = jnp.maximum(highest, jnp.max(logits, axis=0, keepdims=True))
            exponent = jnp.exp2(logits - higher)
            shrink = jnp.exp2(highest - higher)
            acc[cols, :] = acc[cols, :] * shrink + plain(
                vt_ref[cols, rows], exponent.astype(BF16)
            )
            kept.append((higher, summed * shrink + jnp.sum(exponent, axis=0, keepdims=True)))
        return tuple(kept)

    start = (jnp.full(seg_query.shape, MASKED, F32), jnp.zeros(seg_query.shape, F32))
    totals = lax.fori_loop(bounds[0, block], bounds[1, block], step, (start,) * heads)
    for head in range(heads):
        highest, summed = totals[head]
        cols = slice(head * HEAD, (head + 1) * HEAD)
        acc[cols, :] = acc[cols, :] / summed
        lse_ref[head : head + 1, :] = highest + jnp.log2(summed)
    o_ref[...] = acc[...].T.astype(BF16)


def backward_kernel(
    bounds, q_ref, do_ref, k_ref, kt_ref, v_ref, segk_ref, segq_ref, lse_ref, inner_ref,
    dq_ref, dk_ref, dv_ref, dqt, dk_acc, dv_acc,
):
    block = pl.program_id(0)
    heads = lse_ref.shape[0]

    @pl.when(block == 0)
    def _():
        dqt[...] = jnp.zeros_like(dqt)

    dk_acc[...] = jnp.zeros_like(dk_acc)
    dv_acc[...] = jnp.zeros_like(dv_acc)
    seg_key = segk_ref[...]

    def step(tile, carry):
        rows = pl.ds(pl.multiple_of(tile * BQ, BQ), BQ)
        allowed = seg_key == segq_ref[:, rows]
        for head in range(heads):
            cols = slice(head * HEAD, (head + 1) * HEAD)
            queries = q_ref[rows, cols]
            grads = do_ref[rows, cols]
            logits = times_transpose(k_ref[:, cols], queries) * SCALE2
            probs = jnp.exp2(logits - lse_ref[head : head + 1, rows])
            probs = jnp.where(allowed, probs, 0.0)
            grad_probs = times_transpose(v_ref[:, cols], grads)
            scores = (probs * (grad_probs - inner_ref[head : head + 1, rows])).astype(BF16)
            dv_acc[head] += plain(probs.astype(BF16), grads)
            dk_acc[head] += plain(scores, queries)
            dqt[cols, rows] += plain(kt_ref[cols, :], scores)
        return carry

    lax.fori_loop(bounds[0, block], bounds[1, block], step, 0)
    scale = HEAD ** (-0.5)
    for head in range(heads):
        cols = slice(head * HEAD, (head + 1) * HEAD)
        dk_ref[:, cols] = (dk_acc[head] * scale).astype(BF16)
        dv_ref[:, cols] = dv_acc[head].astype(BF16)

    @pl.when(block == pl.num_programs(0) - 1)
    def _():
        for tile in range(dq_ref.shape[0] // BQ):
            rows = slice(tile * BQ, (tile + 1) * BQ)
            dq_ref[rows, :] = (dqt[:, rows] * scale).T.astype(BF16)


def tile_bounds(seg, own, other):
    tiles = seg.reshape(-1, own)
    first = jnp.sum((seg[None, :] < tiles[:, :1]).astype(jnp.int32), axis=1)
    last = jnp.sum((seg[None, :] <= tiles[:, -1:]).astype(jnp.int32), axis=1)
    return jnp.stack([first // other, (last + other - 1) // other])


def attend(heads, qkv, seg):
    length, part = qkv.shape[0], heads * HEAD
    value_turned = qkv[:, 2 * part :].T
    return pl.pallas_call(
        forward_kernel,
        grid_spec=pltpu.PrefetchScalarGridSpec(
            num_scalar_prefetch=1,
            grid=(length // FQ,),
            in_specs=[
                pl.BlockSpec((FQ, part), lambda i, b: (i, 0)),
                pl.BlockSpec((length, part), lambda i, b: (0, 1)),
                pl.BlockSpec((part, length), lambda i, b: (0, 0)),
                pl.BlockSpec((1, FQ), lambda i, b: (0, i)),
                pl.BlockSpec((length, 1), lambda i, b: (0, 0)),
            ],
            out_specs=[
                pl.BlockSpec((FQ, part), lambda i, b: (i, 0)),
                pl.BlockSpec((heads, FQ), lambda i, b: (0, i)),
            ],
            scratch_shapes=[pltpu.VMEM((part, FQ), F32)],
        ),
        out_shape=[
            jax.ShapeDtypeStruct((length, part), BF16),
            jax.ShapeDtypeStruct((heads, length), F32),
        ],
        compiler_params=pltpu.CompilerParams(vmem_limit_bytes=40 * 2**20),
        cost_estimate=pl.CostEstimate(
            flops=4 * length * length * part, bytes_accessed=8 * length * part,
            transcendentals=length * length * heads,
        ),
        name="attend",
    )(tile_bounds(seg, FQ, FK), qkv, qkv, value_turned, seg[None, :], seg[:, None])


def attend_back(heads, qkv, seg, lse, inner, grads):
    length, part = qkv.shape[0], heads * HEAD
    key_turned = qkv[:, part : 2 * part].T
    return pl.pallas_call(
        backward_kernel,
        grid_spec=pltpu.PrefetchScalarGridSpec(
            num_scalar_prefetch=1,
            grid=(length // BK,),
            in_specs=[
                pl.BlockSpec((length, part), lambda i, b: (0, 0)),
                pl.BlockSpec((length, part), lambda i, b: (0, 0)),
                pl.BlockSpec((BK, part), lambda i, b: (i, 1)),
                pl.BlockSpec((part, BK), lambda i, b: (0, i)),
                pl.BlockSpec((BK, part), lambda i, b: (i, 2)),
                pl.BlockSpec((BK, 1), lambda i, b: (i, 0)),
                pl.BlockSpec((1, length), lambda i, b: (0, 0)),
                pl.BlockSpec((heads, length), lambda i, b: (0, 0)),
                pl.BlockSpec((heads, length), lambda i, b: (0, 0)),
            ],
            out_specs=[
                pl.BlockSpec((length, part), lambda i, b: (0, 0)),
                pl.BlockSpec((BK, part), lambda i, b: (i, 0)),
                pl.BlockSpec((BK, part), lambda i, b: (i, 0)),
            ],
            scratch_shapes=[
                pltpu.VMEM((part, length), F32),
                pltpu.VMEM((heads, BK, HEAD), F32),
                pltpu.VMEM((heads, BK, HEAD), F32),
            ],
        ),
        out_shape=[jax.ShapeDtypeStruct((length, part), BF16)] * 3,
        compiler_params=pltpu.CompilerParams(vmem_limit_bytes=48 * 2**20),
        cost_estimate=pl.CostEstimate(
            flops=10 * length * length * part, bytes_accessed=14 * length * part,
            transcendentals=length * length * heads,
        ),
        name="attend_back",
    )(
        tile_bounds(seg, BK, BQ), qkv, grads, qkv, key_turned, qkv,
        seg[:, None], seg[None, :], lse, inner,
    )


def gelu_parts(act):
    phi = 0.5 * (1.0 + lax.erf(act * 0.7071067811865476))
    bell = jnp.exp(act * act * -0.5) * 0.3989422804014327
    return act * phi, phi + act * bell


def body(tokens, segments, gain_attn, w_qkv, w_attn_out, gain_mlp, w_in, w_mlp, cotangent):
    _, local_rows, width = tokens.shape
    ranks = lax.axis_size("row")
    heads = HEADS // ranks
    part = heads * HEAD
    length = local_rows * ranks

    def gather(array, axis, dim):
        return lax.all_gather(array, axis, axis=dim, tiled=True)

    qkv_matrix = gather(gather(w_qkv, "row", 2), "col", 1).reshape(3 * width, width)
    seg = gather(segments, "row", 1).reshape(length)
    out_full = gather(gather(w_attn_out, "row", 1), "col", 0)
    inner_full = gather(w_in, "row", 2)
    mlp_full = gather(w_mlp, "row", 1)
    act_matrix, gate_matrix = inner_full[0], inner_full[1]
    hidden = inner_full.shape[1]

    def scatter_heads(parts):
        packed = jnp.stack([p.astype(BF16).reshape(local_rows, ranks, part) for p in parts], axis=2)
        packed = packed.transpose(1, 0, 2, 3).reshape(length, len(parts) * part)
        return lax.all_to_all(packed, "row", 0, 0, tiled=True)

    def gather_heads(packed):
        count = packed.shape[1] // part
        moved = lax.all_to_all(packed, "row", 0, 0, tiled=True)
        moved = moved.reshape(ranks, local_rows, count, part).transpose(2, 1, 0, 3)
        return moved.reshape(count, local_rows, width)

    inputs = tokens.astype(F32).reshape(local_rows, width)
    norm_one = layer_norm(inputs, gain_attn).astype(BF16)
    projected = times_transpose(norm_one, qkv_matrix)
    positions = (
        lax.axis_index("row") * local_rows + jnp.arange(local_rows, dtype=jnp.int32)
    ).astype(F32)
    cosine, sine = rotary(positions, HEADS)

    def rope(flat):
        return flat * cosine + turned(flat) * sine

    def rope_back(flat):
        return flat * cosine - turned(flat) * sine

    qkv = scatter_heads(
        [rope(projected[:, :width]), rope(projected[:, width : 2 * width]), projected[:, 2 * width :]]
    )
    attended, lse = attend(heads, qkv, seg)
    mixed = gather_heads(attended)[0]
    residual = inputs + times_transpose(mixed, out_full)
    norm_two = layer_norm(residual, gain_mlp).astype(BF16)
    mlp_inputs = gather(norm_two, "col", 0)
    mlp_cot = gather(cotangent.reshape(local_rows, width), "col", 0)

    act = times_transpose(mlp_inputs, act_matrix)
    gate = times_transpose(mlp_inputs, gate_matrix)
    grad_gated = times_transpose(mlp_cot, mlp_full)
    bent, slope = gelu_parts(act)
    gated = (bent * gate).astype(BF16)
    grad_act = (grad_gated * slope * gate).astype(BF16)
    grad_gate = (grad_gated * bent).astype(BF16)

    def over_col(array):
        return lax.psum_scatter(array.astype(BF16), "col", scatter_dimension=0, tiled=True)

    grad_norm_two = over_col(plain(grad_act, act_matrix) + plain(grad_gate, gate_matrix)).astype(F32)
    mlp_out = over_col(plain(gated, mlp_full)).astype(F32)
    output = (residual + mlp_out).astype(BF16).reshape(tokens.shape)

    second_back = jax.vjp(layer_norm, residual, gain_mlp)[1]
    grad_resid_part, grad_gain_mlp = second_back(grad_norm_two)
    grad_residual = cotangent.reshape(local_rows, width).astype(F32) + grad_resid_part
    grad_resid_low = grad_residual.astype(BF16)
    grad_mixed = scatter_heads([plain(grad_resid_low, out_full)])
    inner = jnp.sum(
        (grad_mixed.astype(F32) * attended.astype(F32)).reshape(length, heads, HEAD), axis=-1
    ).T
    back = attend_back(heads, qkv, seg, lse, inner, grad_mixed)

    def over_dp(array):
        return lax.psum_scatter(array.astype(BF16), "dp", scatter_dimension=0, tiled=True)

    def finish(array):
        owned = lax.psum_scatter(array, "row", scatter_dimension=1, tiled=True)
        return gather(owned, "dp", 0).astype(F32)

    grad_mlp_part = over_dp(contract_rows(gated, mlp_cot))
    grad_act_part = over_dp(contract_rows(grad_act, mlp_inputs))
    grad_gate_part = over_dp(contract_rows(grad_gate, mlp_inputs))
    grad_out_part = over_dp(over_col(contract_rows(grad_resid_low, mixed)))

    grad_raw = gather_heads(jnp.concatenate(back, axis=1)).astype(F32)
    grad_projected = jnp.concatenate(
        [rope_back(grad_raw[0]), rope_back(grad_raw[1]), grad_raw[2]], axis=1
    ).astype(BF16)
    grad_qkv = contract_rows(grad_projected, norm_one).astype(BF16)
    grad_qkv = lax.psum_scatter(
        grad_qkv.reshape(3, width, width), "col", scatter_dimension=1, tiled=True
    )
    grad_qkv_part = over_dp(grad_qkv.reshape(-1, width))
    grad_norm_one = plain(grad_projected, qkv_matrix)
    first_back = jax.vjp(layer_norm, inputs, gain_attn)[1]
    grad_in_part, grad_gain_attn = first_back(grad_norm_one)
    grad_input = (grad_residual + grad_in_part).astype(BF16).reshape(tokens.shape)

    grad_w_qkv = finish(grad_qkv_part).reshape(w_qkv.shape)
    grad_w_out = finish(grad_out_part)
    grad_w_in = jnp.stack([finish(grad_act_part), finish(grad_gate_part)])
    grad_w_mlp = finish(grad_mlp_part)
    gains = lax.psum(jnp.stack([grad_gain_attn, grad_gain_mlp]), ("dp", "row", "col"))
    size = width // (ranks * lax.axis_size("col"))
    place = (lax.axis_index("row") * lax.axis_size("col") + lax.axis_index("col")) * size
    gains = lax.dynamic_slice_in_dim(gains, place, size, axis=1)
    return (
        output, grad_input, grad_w_qkv, grad_w_out, grad_w_in, grad_w_mlp, gains[0], gains[1],
    )


def solution(mesh):
    return jax.shard_map(
        body,
        mesh=mesh,
        in_specs=(
            P(("dp", "col"), "row", None),
            P(("dp", "col"), "row"),
            P(),
            P(None, "col", "row"),
            P("col", "row"),
            P(),
            P(None, "col", "row"),
            P("col", "row"),
            P(("dp", "col"), "row", None),
        ),
        out_specs=(
            P(("dp", "col"), "row", None),
            P(("dp", "col"), "row", None),
            P(None, "col", "row"),
            P("col", "row"),
            P(None, "col", "row"),
            P("col", "row"),
            P(("row", "col")),
            P(("row", "col")),
        ),
        check_vma=False,
    )
```

```python
import jax
import jax.numpy as jnp
from jax import lax
from jax.experimental import pallas as pl
from jax.experimental.pallas import tpu as pltpu
from jax.sharding import PartitionSpec as P

HEADS = 16
HEAD = 64
EPSILON = 1e-05
ROPE_BASE = 160000.0
MASKED = -1e30
LOG2E = 1.4426950408889634
SCALE2 = HEAD ** (-0.5) * LOG2E
F32 = jnp.float32
BF16 = jnp.bfloat16
FQ, FK = 256, 512
BK, BQ = 256, 512


def layer_norm(inputs, gain):
    average = jnp.mean(inputs, axis=-1, keepdims=True)
    centred = inputs - average
    variance = jnp.mean(centred * centred, axis=-1, keepdims=True)
    return centred * lax.rsqrt(variance + EPSILON) * gain


def rotary(positions, heads):
    half_head = HEAD // 2
    frequency = jnp.power(ROPE_BASE, -2.0 * jnp.arange(half_head).astype(F32) / HEAD)
    angles = positions[:, None] * frequency[None, :]
    return (jnp.tile(jnp.cos(angles), (1, 2 * heads)), jnp.tile(jnp.sin(angles), (1, 2 * heads)))


def turned(flat):
    half = HEAD // 2
    ahead = jnp.concatenate([flat[:, half:], flat[:, :half]], axis=1)
    behind = jnp.concatenate([flat[:, -half:], flat[:, :-half]], axis=1)
    first = (lax.broadcasted_iota(jnp.int32, flat.shape, 1) % HEAD) < half
    return jnp.where(first, -ahead, behind)


def contract_rows(left_side, right_side):
    return lax.dot_general(
        left_side, right_side, (((0,), (0,)), ((), ())), preferred_element_type=F32
    )


def times_transpose(left_side, right_side):
    return lax.dot_general(
        left_side, right_side, (((1,), (1,)), ((), ())), preferred_element_type=F32
    )


def plain(left_side, right_side):
    return jnp.dot(left_side, right_side, preferred_element_type=F32)


def forward_kernel(bounds, q_ref, k_ref, vt_ref, segq_ref, segk_ref, o_ref, lse_ref, acc):
    block = pl.program_id(0)
    heads = lse_ref.shape[0]
    acc[...] = jnp.zeros_like(acc)
    seg_query = segq_ref[...]

    def step(tile, carry):
        rows = pl.ds(pl.multiple_of(tile * FK, FK), FK)
        allowed = segk_ref[rows, :] == seg_query
        spans = [slice(head * HEAD, (head + 1) * HEAD) for head in range(heads)]
        logits = [
            jnp.where(
                allowed, times_transpose(k_ref[rows, cols], q_ref[:, cols]) * SCALE2, MASKED
            )
            for cols in spans
        ]
        higher = [
            jnp.maximum(carry[head][0], jnp.max(logits[head], axis=0, keepdims=True))
            for head in range(heads)
        ]
        exponents = [jnp.exp2(logits[head] - higher[head]) for head in range(heads)]
        shrink = [jnp.exp2(carry[head][0] - higher[head]) for head in range(heads)]
        sums = [
            carry[head][1] * shrink[head] + jnp.sum(exponents[head], axis=0, keepdims=True)
            for head in range(heads)
        ]
        terms = [
            plain(vt_ref[cols, rows], exponents[head].astype(BF16))
            for head, cols in enumerate(spans)
        ]
        for head, cols in enumerate(spans):
            acc[cols, :] = acc[cols, :] * shrink[head] + terms[head]
        return tuple(zip(higher, sums))

    start = (jnp.full(seg_query.shape, MASKED, F32), jnp.zeros(seg_query.shape, F32))
    totals = lax.fori_loop(bounds[0, block], bounds[1, block], step, (start,) * heads)
    for head in range(heads):
        highest, summed = totals[head]
        cols = slice(head * HEAD, (head + 1) * HEAD)
        acc[cols, :] = acc[cols, :] / summed
        lse_ref[head : head + 1, :] = highest + jnp.log2(summed)
    o_ref[...] = acc[...].T.astype(BF16)


def backward_kernel(
    bounds, q_ref, do_ref, k_ref, kt_ref, v_ref, segk_ref, segq_ref, lse_ref, inner_ref,
    dq_ref, dk_ref, dv_ref, dqt, dk_acc, dv_acc,
):
    block = pl.program_id(0)
    heads = lse_ref.shape[0]

    @pl.when(block == 0)
    def _():
        dqt[...] = jnp.zeros_like(dqt)

    dk_acc[...] = jnp.zeros_like(dk_acc)
    dv_acc[...] = jnp.zeros_like(dv_acc)
    seg_key = segk_ref[...]

    def step(tile, carry):
        rows = pl.ds(pl.multiple_of(tile * BQ, BQ), BQ)
        allowed = seg_key == segq_ref[:, rows]
        for head in range(heads):
            cols = slice(head * HEAD, (head + 1) * HEAD)
            queries = q_ref[rows, cols]
            grads = do_ref[rows, cols]
            logits = times_transpose(k_ref[:, cols], queries) * SCALE2
            probs = jnp.exp2(logits - lse_ref[head : head + 1, rows])
            probs = jnp.where(allowed, probs, 0.0)
            grad_probs = times_transpose(v_ref[:, cols], grads)
            scores = (probs * (grad_probs - inner_ref[head : head + 1, rows])).astype(BF16)
            dv_acc[head] += plain(probs.astype(BF16), grads)
            dk_acc[head] += plain(scores, queries)
            dqt[cols, rows] += plain(kt_ref[cols, :], scores)
        return carry

    lax.fori_loop(bounds[0, block], bounds[1, block], step, 0)
    scale = HEAD ** (-0.5)
    for head in range(heads):
        cols = slice(head * HEAD, (head + 1) * HEAD)
        dk_ref[:, cols] = (dk_acc[head] * scale).astype(BF16)
        dv_ref[:, cols] = dv_acc[head].astype(BF16)

    @pl.when(block == pl.num_programs(0) - 1)
    def _():
        for tile in range(dq_ref.shape[0] // BQ):
            rows = slice(tile * BQ, (tile + 1) * BQ)
            dq_ref[rows, :] = (dqt[:, rows] * scale).T.astype(BF16)


def tile_bounds(seg, own, other):
    tiles = seg.reshape(-1, own)
    first = jnp.sum((seg[None, :] < tiles[:, :1]).astype(jnp.int32), axis=1)
    last = jnp.sum((seg[None, :] <= tiles[:, -1:]).astype(jnp.int32), axis=1)
    return jnp.stack([first // other, (last + other - 1) // other])


def attend(heads, qkv, seg):
    length, part = qkv.shape[0], heads * HEAD
    value_turned = qkv[:, 2 * part :].T
    return pl.pallas_call(
        forward_kernel,
        grid_spec=pltpu.PrefetchScalarGridSpec(
            num_scalar_prefetch=1,
            grid=(length // FQ,),
            in_specs=[
                pl.BlockSpec((FQ, part), lambda i, b: (i, 0)),
                pl.BlockSpec((length, part), lambda i, b: (0, 1)),
                pl.BlockSpec((part, length), lambda i, b: (0, 0)),
                pl.BlockSpec((1, FQ), lambda i, b: (0, i)),
                pl.BlockSpec((length, 1), lambda i, b: (0, 0)),
            ],
            out_specs=[
                pl.BlockSpec((FQ, part), lambda i, b: (i, 0)),
                pl.BlockSpec((heads, FQ), lambda i, b: (0, i)),
            ],
            scratch_shapes=[pltpu.VMEM((part, FQ), F32)],
        ),
        out_shape=[
            jax.ShapeDtypeStruct((length, part), BF16),
            jax.ShapeDtypeStruct((heads, length), F32),
        ],
        compiler_params=pltpu.CompilerParams(vmem_limit_bytes=40 * 2**20),
        cost_estimate=pl.CostEstimate(
            flops=4 * length * length * part, bytes_accessed=8 * length * part,
            transcendentals=length * length * heads,
        ),
        name="attend",
    )(tile_bounds(seg, FQ, FK), qkv, qkv, value_turned, seg[None, :], seg[:, None])


def attend_back(heads, qkv, seg, lse, inner, grads):
    length, part = qkv.shape[0], heads * HEAD
    key_turned = qkv[:, part : 2 * part].T
    return pl.pallas_call(
        backward_kernel,
        grid_spec=pltpu.PrefetchScalarGridSpec(
            num_scalar_prefetch=1,
            grid=(length // BK,),
            in_specs=[
                pl.BlockSpec((length, part), lambda i, b: (0, 0)),
                pl.BlockSpec((length, part), lambda i, b: (0, 0)),
                pl.BlockSpec((BK, part), lambda i, b: (i, 1)),
                pl.BlockSpec((part, BK), lambda i, b: (0, i)),
                pl.BlockSpec((BK, part), lambda i, b: (i, 2)),
                pl.BlockSpec((BK, 1), lambda i, b: (i, 0)),
                pl.BlockSpec((1, length), lambda i, b: (0, 0)),
                pl.BlockSpec((heads, length), lambda i, b: (0, 0)),
                pl.BlockSpec((heads, length), lambda i, b: (0, 0)),
            ],
            out_specs=[
                pl.BlockSpec((length, part), lambda i, b: (0, 0)),
                pl.BlockSpec((BK, part), lambda i, b: (i, 0)),
                pl.BlockSpec((BK, part), lambda i, b: (i, 0)),
            ],
            scratch_shapes=[
                pltpu.VMEM((part, length), F32),
                pltpu.VMEM((heads, BK, HEAD), F32),
                pltpu.VMEM((heads, BK, HEAD), F32),
            ],
        ),
        out_shape=[jax.ShapeDtypeStruct((length, part), BF16)] * 3,
        compiler_params=pltpu.CompilerParams(vmem_limit_bytes=48 * 2**20),
        cost_estimate=pl.CostEstimate(
            flops=10 * length * length * part, bytes_accessed=14 * length * part,
            transcendentals=length * length * heads,
        ),
        name="attend_back",
    )(
        tile_bounds(seg, BK, BQ), qkv, grads, qkv, key_turned, qkv,
        seg[:, None], seg[None, :], lse, inner,
    )


def gelu_parts(act):
    phi = 0.5 * (1.0 + lax.erf(act * 0.7071067811865476))
    bell = jnp.exp(act * act * -0.5) * 0.3989422804014327
    return act * phi, phi + act * bell


def swap(array, bit):
    pairs = [(index, index ^ bit) for index in range(lax.axis_size("dp"))]
    return lax.ppermute(array, "dp", pairs)


def gather_first(piece):
    half = piece.shape[1] // 2
    left, right = piece[:, :half], piece[:, half:]
    return jnp.stack([left, swap(left, 1)]), jnp.stack([right, swap(right, 2)])


def gather_second(pairs):
    left, right = pairs
    return left, right, swap(left, 2), swap(right, 1)


def gather_order(parts):
    own = lax.axis_index("dp")
    left, right, left_far, right_far = parts
    near = jnp.concatenate(
        [
            jnp.concatenate([left, left_far]),
            jnp.stack([right[0], right_far[0], right[1], right_far[1]]),
        ],
        axis=2,
    )
    return jnp.concatenate(
        [lax.dynamic_slice_in_dim(near, index ^ own, 1) for index in range(4)]
    )


def gather_dp(piece):
    return gather_order(gather_second(gather_first(piece)))


def scatter_first(blocks):
    half = blocks.shape[2] // 2
    own = lax.axis_index("dp")
    sides = []
    for start, (first, second) in ((0, (1, 2)), (half, (2, 1))):
        def block(index):
            return lax.dynamic_slice(
                blocks, (index ^ own, 0, start), (1, blocks.shape[1], half)
            )
        far = swap(jnp.concatenate([block(first), block(3)]), first)
        near = block(0).astype(F32) + far[:1].astype(F32)
        passed = (block(second).astype(F32) + far[1:].astype(F32)).astype(BF16)
        sides.append((near, passed))
    return sides


def scatter_second(sides):
    (near_a, passed_a), (near_b, passed_b) = sides
    sums = [near_a + swap(passed_a, 2).astype(F32), near_b + swap(passed_b, 1).astype(F32)]
    return jnp.concatenate([part.astype(BF16) for part in sums], axis=2)[0]


def body(tokens, segments, gain_attn, w_qkv, w_attn_out, gain_mlp, w_in, w_mlp, cotangent):
    _, local_rows, width = tokens.shape
    ranks = lax.axis_size("row")
    heads = HEADS // ranks
    part = heads * HEAD
    length = local_rows * ranks

    def gather(array, axis, dim):
        return lax.all_gather(array, axis, axis=dim, tiled=True)

    cols = lax.axis_size("col")
    own_dp = lax.axis_index("dp")

    def own_rows(array, dim):
        size = array.shape[dim] // 4
        return lax.dynamic_slice_in_dim(array, own_dp * size, size, axis=dim)

    hidden = w_mlp.shape[0]
    out_rows = w_attn_out.shape[0]
    quarter, out_quarter = hidden // 4, out_rows // 4
    seg = gather(segments, "row", 1).reshape(length)
    tokens, seg = lax.optimization_barrier((tokens, seg))
    qkv_rows = gather(own_rows(w_qkv, 1).reshape(-1, w_qkv.shape[2]), "row", 1)
    rest = jnp.concatenate(
        [own_rows(w_in, 1).reshape(2 * quarter, -1), own_rows(w_mlp, 0), own_rows(w_attn_out, 0)]
    )
    rest, qkv_rows = lax.optimization_barrier((rest, qkv_rows))
    qkv_near = gather_dp(qkv_rows).reshape(4, 3, out_quarter, width)
    qkv_near = qkv_near.transpose(1, 0, 2, 3).reshape(3, out_rows, width)
    qkv_matrix = gather(qkv_near, "col", 1).reshape(3 * width, width)
    rest, qkv_late = lax.optimization_barrier((gather(rest, "row", 1), qkv_matrix))
    rest_pairs = gather_first(rest)

    def scatter_heads(parts):
        packed = jnp.stack([p.astype(BF16).reshape(local_rows, ranks, part) for p in parts], axis=2)
        packed = packed.transpose(1, 0, 2, 3).reshape(length, len(parts) * part)
        return lax.all_to_all(packed, "row", 0, 0, tiled=True)

    def gather_heads(packed):
        count = packed.shape[1] // part
        moved = lax.all_to_all(packed, "row", 0, 0, tiled=True)
        moved = moved.reshape(ranks, local_rows, count, part).transpose(2, 1, 0, 3)
        return moved.reshape(count, local_rows, width)

    inputs = tokens.astype(F32).reshape(local_rows, width)
    norm_one = layer_norm(inputs, gain_attn).astype(BF16)
    projected = times_transpose(norm_one, qkv_matrix)
    positions = (
        lax.axis_index("row") * local_rows + jnp.arange(local_rows, dtype=jnp.int32)
    ).astype(F32)
    cosine, sine = rotary(positions, HEADS)

    def rope(flat):
        return flat * cosine + turned(flat) * sine

    def rope_back(flat):
        return flat * cosine - turned(flat) * sine

    qkv = scatter_heads(
        [rope(projected[:, :width]), rope(projected[:, width : 2 * width]), projected[:, 2 * width :]]
    )
    rest_pairs, qkv = lax.optimization_barrier((rest_pairs, qkv))
    rest_parts = gather_second(rest_pairs)
    attended, lse = attend(heads, qkv, seg)
    rest_parts, attended = lax.optimization_barrier((rest_parts, attended))
    rest = gather_order(rest_parts)
    act_matrix = rest[:, :quarter].reshape(hidden, width)
    gate_matrix = rest[:, quarter : 2 * quarter].reshape(hidden, width)
    mlp_full = rest[:, 2 * quarter : 3 * quarter].reshape(hidden, width)
    out_full = gather(rest[:, 3 * quarter :].reshape(out_rows, width), "col", 0)
    mixed = gather_heads(attended)[0]
    residual = inputs + times_transpose(mixed, out_full)
    norm_two = layer_norm(residual, gain_mlp).astype(BF16)
    mlp_inputs = gather(norm_two, "col", 0)
    mlp_cot = gather(cotangent.reshape(local_rows, width), "col", 0)

    act = times_transpose(mlp_inputs, act_matrix)
    gate = times_transpose(mlp_inputs, gate_matrix)
    grad_gated = times_transpose(mlp_cot, mlp_full)
    bent, slope = gelu_parts(act)
    gated = (bent * gate).astype(BF16)
    grad_act = (grad_gated * slope * gate).astype(BF16)
    grad_gate = (grad_gated * bent).astype(BF16)

    def over_col(array):
        return lax.psum_scatter(array.astype(BF16), "col", scatter_dimension=0, tiled=True)

    grad_norm_two = over_col(plain(grad_act, act_matrix) + plain(grad_gate, gate_matrix)).astype(F32)
    mlp_out = over_col(plain(gated, mlp_full)).astype(F32)
    output = (residual + mlp_out).astype(BF16).reshape(tokens.shape)

    second_back = jax.vjp(layer_norm, residual, gain_mlp)[1]
    grad_resid_part, grad_gain_mlp = second_back(grad_norm_two)
    grad_residual = cotangent.reshape(local_rows, width).astype(F32) + grad_resid_part
    grad_resid_low = grad_residual.astype(BF16)
    grad_mixed = scatter_heads([plain(grad_resid_low, out_full)])
    inner = jnp.sum(
        (grad_mixed.astype(F32) * attended.astype(F32)).reshape(length, heads, HEAD), axis=-1
    ).T
    mlp_grads = [
        contract_rows(grad_act, mlp_inputs),
        contract_rows(grad_gate, mlp_inputs),
        contract_rows(gated, mlp_cot),
    ]
    mlp_sides = scatter_first(
        jnp.concatenate([g.astype(BF16).reshape(4, quarter, width) for g in mlp_grads], axis=1)
    )
    mlp_sides, grad_mixed = lax.optimization_barrier((mlp_sides, grad_mixed))
    back = attend_back(heads, qkv, seg, lse, inner, grad_mixed)
    mlp_owned, back = lax.optimization_barrier((scatter_second(mlp_sides), back))

    def finish(owned):
        return gather_dp(lax.psum_scatter(owned, "row", scatter_dimension=1, tiled=True)).astype(F32)

    grad_raw = gather_heads(jnp.concatenate(back, axis=1)).astype(F32)
    mlp_owned, grad_raw = lax.optimization_barrier((mlp_owned, grad_raw))
    mlp_sums = finish(mlp_owned)
    mlp_sums = [
        mlp_sums[:, index * quarter : (index + 1) * quarter].reshape(hidden, -1) for index in range(3)
    ]
    grad_w_in, grad_w_mlp = jnp.stack(mlp_sums[:2]), mlp_sums[2]
    grad_w_out = contract_rows(grad_resid_low, mixed).astype(BF16)

    grad_projected = jnp.concatenate(
        [rope_back(grad_raw[0]), rope_back(grad_raw[1]), grad_raw[2]], axis=1
    ).astype(BF16)
    grad_qkv = contract_rows(grad_projected, norm_one).astype(BF16)
    grad_norm_one = plain(grad_projected, qkv_late)
    first_back = jax.vjp(layer_norm, inputs, gain_attn)[1]
    grad_in_part, grad_gain_attn = first_back(grad_norm_one)
    grad_input = (grad_residual + grad_in_part).astype(BF16).reshape(tokens.shape)

    size = width // (ranks * cols)
    gains = jnp.stack([grad_gain_attn, grad_gain_mlp]).astype(BF16)
    gains = gains.reshape(2, ranks, cols, size).transpose(2, 1, 0, 3).reshape(cols, ranks, 2 * size)
    gains = jnp.pad(gains, ((0, 0), (0, 0), (0, width // ranks - 2 * size)))
    gains = jnp.pad(gains.reshape(cols, 1, 1, width), ((0, 0), (0, 3), (0, 15), (0, 0)))
    packed = jnp.concatenate(
        [
            grad_qkv.reshape(3, cols, 4, out_quarter, width)
            .transpose(1, 2, 0, 3, 4)
            .reshape(cols, 4, 3 * out_quarter, width),
            grad_w_out.reshape(cols, 4, out_quarter, width),
            gains,
        ],
        axis=2,
    )
    packed = lax.psum_scatter(packed, "col", scatter_dimension=0, tiled=True)[0]
    sums = finish(scatter_second(scatter_first(packed)))
    grad_w_qkv = sums[:, : 3 * out_quarter].reshape(4, 3, out_quarter, -1)
    grad_w_qkv = grad_w_qkv.transpose(1, 0, 2, 3).reshape(w_qkv.shape)
    grad_w_out = sums[:, 3 * out_quarter : 4 * out_quarter].reshape(w_attn_out.shape)
    gains = sums[0, 4 * out_quarter, : 2 * size].reshape(2, size)
    return (
        output, grad_input, grad_w_qkv, grad_w_out, grad_w_in, grad_w_mlp, gains[0], gains[1],
    )


def solution(mesh):
    return jax.shard_map(
        body,
        mesh=mesh,
        in_specs=(
            P(("dp", "col"), "row", None),
            P(("dp", "col"), "row"),
            P(),
            P(None, "col", "row"),
            P("col", "row"),
            P(),
            P(None, "col", "row"),
            P("col", "row"),
            P(("dp", "col"), "row", None),
        ),
        out_specs=(
            P(("dp", "col"), "row", None),
            P(("dp", "col"), "row", None),
            P(None, "col", "row"),
            P("col", "row"),
            P(None, "col", "row"),
            P("col", "row"),
            P(("row", "col")),
            P(("row", "col")),
        ),
        check_vma=False,
    )
```

```python
import jax
import jax.numpy as jnp
from jax import lax
from jax.experimental import pallas as pl
from jax.experimental.pallas import tpu as pltpu
from jax.sharding import PartitionSpec as P

HEADS = 16
HEAD = 64
EPSILON = 1e-05
ROPE_BASE = 160000.0
MASKED = -1e30
LOG2E = 1.4426950408889634
SCALE2 = HEAD ** (-0.5) * LOG2E
F32 = jnp.float32
BF16 = jnp.bfloat16
FQ, FK = 256, 512
BK, BQ = 256, 512


def layer_norm(inputs, gain):
    average = jnp.mean(inputs, axis=-1, keepdims=True)
    centred = inputs - average
    variance = jnp.mean(centred * centred, axis=-1, keepdims=True)
    return centred * lax.rsqrt(variance + EPSILON) * gain


def rotary(positions, heads):
    half_head = HEAD // 2
    frequency = jnp.power(ROPE_BASE, -2.0 * jnp.arange(half_head).astype(F32) / HEAD)
    angles = positions[:, None] * frequency[None, :]
    return (jnp.tile(jnp.cos(angles), (1, 2 * heads)), jnp.tile(jnp.sin(angles), (1, 2 * heads)))


def turned(flat):
    half = HEAD // 2
    ahead = jnp.concatenate([flat[:, half:], flat[:, :half]], axis=1)
    behind = jnp.concatenate([flat[:, -half:], flat[:, :-half]], axis=1)
    first = (lax.broadcasted_iota(jnp.int32, flat.shape, 1) % HEAD) < half
    return jnp.where(first, -ahead, behind)


def contract_rows(left_side, right_side):
    return lax.dot_general(
        left_side, right_side, (((0,), (0,)), ((), ())), preferred_element_type=F32
    )


def times_transpose(left_side, right_side):
    return lax.dot_general(
        left_side, right_side, (((1,), (1,)), ((), ())), preferred_element_type=F32
    )


def plain(left_side, right_side):
    return jnp.dot(left_side, right_side, preferred_element_type=F32)


def forward_kernel(bounds, q_ref, k_ref, vt_ref, segq_ref, segk_ref, o_ref, lse_ref, acc):
    block = pl.program_id(0)
    heads = lse_ref.shape[0]
    acc[...] = jnp.zeros_like(acc)
    seg_query = segq_ref[...]

    def step(tile, carry):
        rows = pl.ds(pl.multiple_of(tile * FK, FK), FK)
        allowed = segk_ref[rows, :] == seg_query
        spans = [slice(head * HEAD, (head + 1) * HEAD) for head in range(heads)]
        logits = [
            jnp.where(
                allowed, times_transpose(k_ref[rows, cols], q_ref[:, cols]) * SCALE2, MASKED
            )
            for cols in spans
        ]
        higher = [
            jnp.maximum(carry[head][0], jnp.max(logits[head], axis=0, keepdims=True))
            for head in range(heads)
        ]
        exponents = [jnp.exp2(logits[head] - higher[head]) for head in range(heads)]
        shrink = [jnp.exp2(carry[head][0] - higher[head]) for head in range(heads)]
        sums = [
            carry[head][1] * shrink[head] + jnp.sum(exponents[head], axis=0, keepdims=True)
            for head in range(heads)
        ]
        terms = [
            plain(vt_ref[cols, rows], exponents[head].astype(BF16))
            for head, cols in enumerate(spans)
        ]
        for head, cols in enumerate(spans):
            acc[cols, :] = acc[cols, :] * shrink[head] + terms[head]
        return tuple(zip(higher, sums))

    start = (jnp.full(seg_query.shape, MASKED, F32), jnp.zeros(seg_query.shape, F32))
    totals = lax.fori_loop(bounds[0, block], bounds[1, block], step, (start,) * heads)
    for head in range(heads):
        highest, summed = totals[head]
        cols = slice(head * HEAD, (head + 1) * HEAD)
        acc[cols, :] = acc[cols, :] / summed
        lse_ref[head : head + 1, :] = highest + jnp.log2(summed)
    o_ref[...] = acc[...].T.astype(BF16)


def backward_kernel(
    bounds, q_ref, do_ref, k_ref, kt_ref, v_ref, segk_ref, segq_ref, lse_ref, inner_ref,
    dq_ref, dk_ref, dv_ref, dqt, dk_acc, dv_acc,
):
    block = pl.program_id(0)
    heads = lse_ref.shape[0]

    @pl.when(block == 0)
    def _():
        dqt[...] = jnp.zeros_like(dqt)

    dk_acc[...] = jnp.zeros_like(dk_acc)
    dv_acc[...] = jnp.zeros_like(dv_acc)
    seg_key = segk_ref[...]

    def step(tile, carry):
        rows = pl.ds(pl.multiple_of(tile * BQ, BQ), BQ)
        allowed = seg_key == segq_ref[:, rows]
        for head in range(heads):
            cols = slice(head * HEAD, (head + 1) * HEAD)
            queries = q_ref[rows, cols]
            grads = do_ref[rows, cols]
            logits = times_transpose(k_ref[:, cols], queries) * SCALE2
            probs = jnp.exp2(logits - lse_ref[head : head + 1, rows])
            probs = jnp.where(allowed, probs, 0.0)
            grad_probs = times_transpose(v_ref[:, cols], grads)
            scores = (probs * (grad_probs - inner_ref[head : head + 1, rows])).astype(BF16)
            dv_acc[head] += plain(probs.astype(BF16), grads)
            dk_acc[head] += plain(scores, queries)
            dqt[cols, rows] += plain(kt_ref[cols, :], scores)
        return carry

    lax.fori_loop(bounds[0, block], bounds[1, block], step, 0)
    scale = HEAD ** (-0.5)
    for head in range(heads):
        cols = slice(head * HEAD, (head + 1) * HEAD)
        dk_ref[:, cols] = (dk_acc[head] * scale).astype(BF16)
        dv_ref[:, cols] = dv_acc[head].astype(BF16)

    @pl.when(block == pl.num_programs(0) - 1)
    def _():
        for tile in range(dq_ref.shape[0] // BQ):
            rows = slice(tile * BQ, (tile + 1) * BQ)
            dq_ref[rows, :] = (dqt[:, rows] * scale).T.astype(BF16)


def tile_bounds(seg, own, other):
    tiles = seg.reshape(-1, own)
    first = jnp.sum((seg[None, :] < tiles[:, :1]).astype(jnp.int32), axis=1)
    last = jnp.sum((seg[None, :] <= tiles[:, -1:]).astype(jnp.int32), axis=1)
    return jnp.stack([first // other, (last + other - 1) // other])


def attend(heads, qkv, seg):
    length, part = qkv.shape[0], heads * HEAD
    value_turned = qkv[:, 2 * part :].T
    return pl.pallas_call(
        forward_kernel,
        grid_spec=pltpu.PrefetchScalarGridSpec(
            num_scalar_prefetch=1,
            grid=(length // FQ,),
            in_specs=[
                pl.BlockSpec((FQ, part), lambda i, b: (i, 0)),
                pl.BlockSpec((length, part), lambda i, b: (0, 1)),
                pl.BlockSpec((part, length), lambda i, b: (0, 0)),
                pl.BlockSpec((1, FQ), lambda i, b: (0, i)),
                pl.BlockSpec((length, 1), lambda i, b: (0, 0)),
            ],
            out_specs=[
                pl.BlockSpec((FQ, part), lambda i, b: (i, 0)),
                pl.BlockSpec((heads, FQ), lambda i, b: (0, i)),
            ],
            scratch_shapes=[pltpu.VMEM((part, FQ), F32)],
        ),
        out_shape=[
            jax.ShapeDtypeStruct((length, part), BF16),
            jax.ShapeDtypeStruct((heads, length), F32),
        ],
        compiler_params=pltpu.CompilerParams(vmem_limit_bytes=40 * 2**20),
        cost_estimate=pl.CostEstimate(
            flops=4 * length * length * part, bytes_accessed=8 * length * part,
            transcendentals=length * length * heads,
        ),
        name="attend",
    )(tile_bounds(seg, FQ, FK), qkv, qkv, value_turned, seg[None, :], seg[:, None])


def attend_back(heads, qkv, seg, lse, inner, grads):
    length, part = qkv.shape[0], heads * HEAD
    key_turned = qkv[:, part : 2 * part].T
    return pl.pallas_call(
        backward_kernel,
        grid_spec=pltpu.PrefetchScalarGridSpec(
            num_scalar_prefetch=1,
            grid=(length // BK,),
            in_specs=[
                pl.BlockSpec((length, part), lambda i, b: (0, 0)),
                pl.BlockSpec((length, part), lambda i, b: (0, 0)),
                pl.BlockSpec((BK, part), lambda i, b: (i, 1)),
                pl.BlockSpec((part, BK), lambda i, b: (0, i)),
                pl.BlockSpec((BK, part), lambda i, b: (i, 2)),
                pl.BlockSpec((BK, 1), lambda i, b: (i, 0)),
                pl.BlockSpec((1, length), lambda i, b: (0, 0)),
                pl.BlockSpec((heads, length), lambda i, b: (0, 0)),
                pl.BlockSpec((heads, length), lambda i, b: (0, 0)),
            ],
            out_specs=[
                pl.BlockSpec((length, part), lambda i, b: (0, 0)),
                pl.BlockSpec((BK, part), lambda i, b: (i, 0)),
                pl.BlockSpec((BK, part), lambda i, b: (i, 0)),
            ],
            scratch_shapes=[
                pltpu.VMEM((part, length), F32),
                pltpu.VMEM((heads, BK, HEAD), F32),
                pltpu.VMEM((heads, BK, HEAD), F32),
            ],
        ),
        out_shape=[jax.ShapeDtypeStruct((length, part), BF16)] * 3,
        compiler_params=pltpu.CompilerParams(vmem_limit_bytes=48 * 2**20),
        cost_estimate=pl.CostEstimate(
            flops=10 * length * length * part, bytes_accessed=14 * length * part,
            transcendentals=length * length * heads,
        ),
        name="attend_back",
    )(
        tile_bounds(seg, BK, BQ), qkv, grads, qkv, key_turned, qkv,
        seg[:, None], seg[None, :], lse, inner,
    )


def gelu_parts(act):
    phi = 0.5 * (1.0 + lax.erf(act * 0.7071067811865476))
    bell = jnp.exp(act * act * -0.5) * 0.3989422804014327
    return act * phi, phi + act * bell


def swap(array, bit):
    pairs = [(index, index ^ bit) for index in range(lax.axis_size("dp"))]
    return lax.ppermute(array, "dp", pairs)


def gather_first(piece):
    half = piece.shape[1] // 2
    left, right = piece[:, :half], piece[:, half:]
    return jnp.stack([left, swap(left, 1)]), jnp.stack([right, swap(right, 2)])


def gather_second(pairs):
    left, right = pairs
    return left, right, swap(left, 2), swap(right, 1)


def gather_order(parts):
    own = lax.axis_index("dp")
    left, right, left_far, right_far = parts
    near = jnp.concatenate(
        [
            jnp.concatenate([left, left_far]),
            jnp.stack([right[0], right_far[0], right[1], right_far[1]]),
        ],
        axis=2,
    )
    return jnp.concatenate(
        [lax.dynamic_slice_in_dim(near, index ^ own, 1) for index in range(4)]
    )


def gather_dp(piece):
    return gather_order(gather_second(gather_first(piece)))


def scatter_first(blocks):
    half = blocks.shape[2] // 2
    own = lax.axis_index("dp")
    routes = ((0, (1, 2)), (half, (2, 1)))

    def block(index, start):
        return lax.dynamic_slice(blocks, (index ^ own, 0, start), (1, blocks.shape[1], half))

    fars = [
        swap(jnp.concatenate([block(first, start), block(3, start)]), first)
        for start, (first, _) in routes
    ]
    fars = lax.optimization_barrier(fars)
    sides = []
    for far, (start, (_, second)) in zip(fars, routes):
        near = block(0, start).astype(F32) + far[:1].astype(F32)
        passed = (block(second, start).astype(F32) + far[1:].astype(F32)).astype(BF16)
        sides.append((near, passed))
    return sides


def scatter_second(sides):
    (near_a, passed_a), (near_b, passed_b) = sides
    sums = [near_a + swap(passed_a, 2).astype(F32), near_b + swap(passed_b, 1).astype(F32)]
    return jnp.concatenate([part.astype(BF16) for part in sums], axis=2)[0]


def body(tokens, segments, gain_attn, w_qkv, w_attn_out, gain_mlp, w_in, w_mlp, cotangent):
    _, local_rows, width = tokens.shape
    ranks = lax.axis_size("row")
    heads = HEADS // ranks
    part = heads * HEAD
    length = local_rows * ranks

    def gather(array, axis, dim):
        return lax.all_gather(array, axis, axis=dim, tiled=True)

    cols = lax.axis_size("col")
    own_dp = lax.axis_index("dp")

    def own_rows(array, dim):
        size = array.shape[dim] // 4
        return lax.dynamic_slice_in_dim(array, own_dp * size, size, axis=dim)

    hidden = w_mlp.shape[0]
    out_rows = w_attn_out.shape[0]
    quarter, out_quarter = hidden // 4, out_rows // 4
    seg = gather(segments, "row", 1).reshape(length)
    tokens, seg = lax.optimization_barrier((tokens, seg))
    qkv_rows = gather(own_rows(w_qkv, 1).reshape(-1, w_qkv.shape[2]), "row", 1)
    rest = jnp.concatenate(
        [own_rows(w_in, 1).reshape(2 * quarter, -1), own_rows(w_mlp, 0), own_rows(w_attn_out, 0)]
    )
    rest, qkv_rows = lax.optimization_barrier((rest, qkv_rows))
    qkv_near = gather_dp(qkv_rows).reshape(4, 3, out_quarter, width)
    qkv_near = qkv_near.transpose(1, 0, 2, 3).reshape(3, out_rows, width)
    qkv_matrix = gather(qkv_near, "col", 1).reshape(3 * width, width)
    rest, qkv_late = lax.optimization_barrier((gather(rest, "row", 1), qkv_matrix))
    rest_pairs = gather_first(rest)

    def scatter_heads(parts):
        packed = jnp.stack([p.astype(BF16).reshape(local_rows, ranks, part) for p in parts], axis=2)
        packed = packed.transpose(1, 0, 2, 3).reshape(length, len(parts) * part)
        return lax.all_to_all(packed, "row", 0, 0, tiled=True)

    def gather_heads(packed):
        count = packed.shape[1] // part
        moved = lax.all_to_all(packed, "row", 0, 0, tiled=True)
        moved = moved.reshape(ranks, local_rows, count, part).transpose(2, 1, 0, 3)
        return moved.reshape(count, local_rows, width)

    inputs = tokens.astype(F32).reshape(local_rows, width)
    norm_one = layer_norm(inputs, gain_attn).astype(BF16)
    projected = times_transpose(norm_one, qkv_matrix)
    positions = (
        lax.axis_index("row") * local_rows + jnp.arange(local_rows, dtype=jnp.int32)
    ).astype(F32)
    cosine, sine = rotary(positions, HEADS)

    def rope(flat):
        return flat * cosine + turned(flat) * sine

    def rope_back(flat):
        return flat * cosine - turned(flat) * sine

    qkv = scatter_heads(
        [rope(projected[:, :width]), rope(projected[:, width : 2 * width]), projected[:, 2 * width :]]
    )
    rest_pairs, qkv = lax.optimization_barrier((rest_pairs, qkv))
    rest_parts = gather_second(rest_pairs)
    attended, lse = attend(heads, qkv, seg)
    rest_parts, attended = lax.optimization_barrier((rest_parts, attended))
    rest = gather_order(rest_parts)
    act_matrix = rest[:, :quarter].reshape(hidden, width)
    gate_matrix = rest[:, quarter : 2 * quarter].reshape(hidden, width)
    mlp_full = rest[:, 2 * quarter : 3 * quarter].reshape(hidden, width)
    out_full = gather(rest[:, 3 * quarter :].reshape(out_rows, width), "col", 0)
    mixed = gather_heads(attended)[0]
    residual = inputs + times_transpose(mixed, out_full)
    norm_two = layer_norm(residual, gain_mlp).astype(BF16)
    mlp_inputs = gather(norm_two, "col", 0)
    mlp_cot = gather(cotangent.reshape(local_rows, width), "col", 0)

    act = times_transpose(mlp_inputs, act_matrix)
    gate = times_transpose(mlp_inputs, gate_matrix)
    grad_gated = times_transpose(mlp_cot, mlp_full)
    bent, slope = gelu_parts(act)
    gated = (bent * gate).astype(BF16)
    grad_act = (grad_gated * slope * gate).astype(BF16)
    grad_gate = (grad_gated * bent).astype(BF16)

    def over_col(array):
        return lax.psum_scatter(array.astype(BF16), "col", scatter_dimension=0, tiled=True)

    grad_norm_two = over_col(plain(grad_act, act_matrix) + plain(grad_gate, gate_matrix)).astype(F32)
    mlp_out = over_col(plain(gated, mlp_full)).astype(F32)
    output = (residual + mlp_out).astype(BF16).reshape(tokens.shape)

    second_back = jax.vjp(layer_norm, residual, gain_mlp)[1]
    grad_resid_part, grad_gain_mlp = second_back(grad_norm_two)
    grad_residual = cotangent.reshape(local_rows, width).astype(F32) + grad_resid_part
    grad_resid_low = grad_residual.astype(BF16)
    grad_mixed = scatter_heads([plain(grad_resid_low, out_full)])
    inner = jnp.sum(
        (grad_mixed.astype(F32) * attended.astype(F32)).reshape(length, heads, HEAD), axis=-1
    ).T
    mlp_grads = [
        contract_rows(grad_act, mlp_inputs),
        contract_rows(grad_gate, mlp_inputs),
        contract_rows(gated, mlp_cot),
    ]
    mlp_sides = scatter_first(
        jnp.concatenate([g.astype(BF16).reshape(4, quarter, width) for g in mlp_grads], axis=1)
    )
    mlp_sides, grad_mixed = lax.optimization_barrier((mlp_sides, grad_mixed))
    back = attend_back(heads, qkv, seg, lse, inner, grad_mixed)
    mlp_owned, back = lax.optimization_barrier((scatter_second(mlp_sides), back))

    def finish(owned):
        return gather_dp(lax.psum_scatter(owned, "row", scatter_dimension=1, tiled=True)).astype(F32)

    grad_raw = gather_heads(jnp.concatenate(back, axis=1))
    mlp_owned, grad_raw = lax.optimization_barrier((mlp_owned, grad_raw))
    grad_raw = grad_raw.astype(F32)
    mlp_sums = finish(mlp_owned)
    mlp_sums = [
        mlp_sums[:, index * quarter : (index + 1) * quarter].reshape(hidden, -1) for index in range(3)
    ]
    grad_w_in, grad_w_mlp = jnp.stack(mlp_sums[:2]), mlp_sums[2]
    grad_w_out = contract_rows(grad_resid_low, mixed).astype(BF16)

    grad_projected = jnp.concatenate(
        [rope_back(grad_raw[0]), rope_back(grad_raw[1]), grad_raw[2]], axis=1
    ).astype(BF16)
    grad_qkv = contract_rows(grad_projected, norm_one).astype(BF16)
    grad_norm_one = plain(grad_projected, qkv_late)
    first_back = jax.vjp(layer_norm, inputs, gain_attn)[1]
    grad_in_part, grad_gain_attn = first_back(grad_norm_one)
    grad_input = (grad_residual + grad_in_part).astype(BF16).reshape(tokens.shape)

    size = width // (ranks * cols)
    gains = jnp.stack([grad_gain_attn, grad_gain_mlp]).astype(BF16)
    gains = gains.reshape(2, ranks, cols, size).transpose(2, 1, 0, 3).reshape(cols, ranks, 2 * size)
    gains = jnp.pad(gains, ((0, 0), (0, 0), (0, width // ranks - 2 * size)))
    gains = jnp.pad(gains.reshape(cols, 1, 1, width), ((0, 0), (0, 3), (0, 15), (0, 0)))
    packed = jnp.concatenate(
        [
            grad_qkv.reshape(3, cols, 4, out_quarter, width)
            .transpose(1, 2, 0, 3, 4)
            .reshape(cols, 4, 3 * out_quarter, width),
            grad_w_out.reshape(cols, 4, out_quarter, width),
            gains,
        ],
        axis=2,
    )
    packed = lax.psum_scatter(packed, "col", scatter_dimension=0, tiled=True)[0]
    sums = finish(scatter_second(scatter_first(packed)))
    grad_w_qkv = sums[:, : 3 * out_quarter].reshape(4, 3, out_quarter, -1)
    grad_w_qkv = grad_w_qkv.transpose(1, 0, 2, 3).reshape(w_qkv.shape)
    grad_w_out = sums[:, 3 * out_quarter : 4 * out_quarter].reshape(w_attn_out.shape)
    gains = sums[0, 4 * out_quarter, : 2 * size].reshape(2, size)
    return (
        output, grad_input, grad_w_qkv, grad_w_out, grad_w_in, grad_w_mlp, gains[0], gains[1],
    )


def solution(mesh):
    return jax.shard_map(
        body,
        mesh=mesh,
        in_specs=(
            P(("dp", "col"), "row", None),
            P(("dp", "col"), "row"),
            P(),
            P(None, "col", "row"),
            P("col", "row"),
            P(),
            P(None, "col", "row"),
            P("col", "row"),
            P(("dp", "col"), "row", None),
        ),
        out_specs=(
            P(("dp", "col"), "row", None),
            P(("dp", "col"), "row", None),
            P(None, "col", "row"),
            P("col", "row"),
            P(None, "col", "row"),
            P("col", "row"),
            P(("row", "col")),
            P(("row", "col")),
        ),
        check_vma=False,
    )
```
